32 devices in a mesh: members: 2 (over y), lon: 4 (over z), lat: 2 (over x), lev: 2 (over core).
Axes of the slice: x: 2, y: 2, z: 4, core: 2. Of those that a mesh axis runs over, the one named last changes fastest.
Arguments:
- ash_density_field: float32 [12, 4, 256, 512], P('members', 'lev', 'lat', 'lon'), parts along dimension 0, may hold values from 0.05 to 5
- face_transport_numbers: float32 [2, 4, 256, 512], P(None, 'lev', 'lat', 'lon'), may hold values from -0.15 to 0.15
- spreading_number: float32 [6, 4], replicated, may hold values from 0.01 to 0.03
- particle_fall_category: int32 [6], replicated, may hold values from 0 to 3
- crater_parallel_position: int32 [8], P('members'), parts along dimension 0, may hold values from 0 to 255
- crater_meridian_position: int32 [8], P('members'), parts along dimension 0, may hold values from 0 to 511
- crater_release_altitude: int32 [8], P('members'), parts along dimension 0, may hold values from 0 to 3
- eruption_source_amount: float32 [8, 6], P('members'), parts along dimension 0, may hold values from 0.5 to 4
- optical_depth_factor: float32 [8, 6], replicated, may hold values from 0.005 to 0.05
- spectral_radiance_share: float32 [8], replicated, may hold values from 0.5 to 2
- atmosphere_warmth: float32 [4, 256, 512], P('lev', 'lat', 'lon'), may hold values from 200 to 290
- ground_warmth_kelvin: float32 [256, 512], P('lat', 'lon'), may hold values from 250 to 310
Outputs:
- settled: float32 [12, 4, 256, 512], P('members', 'lev', 'lat', 'lon'), parts along dimension 0
- upwelling: float32 [16, 4, 256, 512], P('members', 'lev', 'lat', 'lon'), parts along dimension 0
The draws below stay inside these ranges and needn't reach their ends.
There are 2 independent parts, one for each index of `members`. The reference program is written for one: setup_inputs(seed, part) draws one part's arguments, and reference() takes and returns one part's arrays. A program takes and returns all parts, laid end to end along the dimension named above; an argument that names none is the same for every part. Nothing has to cross between parts.
Inputs may be any that keep to these rules, and one draw needn't show every extreme that they name: `particle_fall_category`: a settling class for each grain size. `crater_parallel_position`: vents may share a cell.
All inputs are finite; a program needn't handle non-finite values.
Results may differ from the reference program's by a relative error of at most 0.0001.
Values sent between devices are 32-bit elements; how exact they have to be, the bound alone decides.
A program may use at most 64 MiB of HBM per device.

```python
import math
import jax
import jax.numpy as jnp
from jax import lax

G = 6
NB = 8
NCLASS = 4
NSRC = 4
STEPS = 2
ALTITUDE_TIERS = 4
PARALLEL_BANDS_N = 256
MERIDIAN_SLOTS = 512


def set_ends(array, stream_key, least, top_value):
    index_at = [jax.random.randint(jax.random.fold_in(stream_key, axis), (), 0, length) for axis, length in enumerate(array.shape)]
    longest = array.shape.index(max(array.shape))
    beside = index_at[:longest] + [(index_at[longest] + 1) % array.shape[longest]] + index_at[longest + 1:]
    return array.at[tuple(index_at)].set(least).at[tuple(beside)].set(top_value)


def block_levels(stream_key, shape, cuts, least, top_value):
    factor_of = 1.0
    for position, parts in cuts:
        steps = jax.random.uniform(jax.random.fold_in(jax.random.fold_in(stream_key, 6), position), (parts,), jnp.float32, least / len(cuts), top_value / len(cuts))
        factor_of = factor_of * jnp.repeat(jnp.exp(steps), shape[position] // parts).reshape((-1,) + (1,) * (len(shape) - 1 - position))
    return factor_of


def setup_inputs(seed: int = 0, part: int = 0) -> dict:
    key_list = jax.random.split(jax.random.key(seed), 13)
    own_keys = jax.random.split(jax.random.fold_in(key_list[12], part), 13)
    ash_density_field = jnp.clip(jnp.exp(math.log(5.0) - 4.6051702 * jax.random.uniform(own_keys[0], (G, ALTITUDE_TIERS, PARALLEL_BANDS_N, MERIDIAN_SLOTS), jnp.float32) ** block_levels(own_keys[0], (G, ALTITUDE_TIERS, PARALLEL_BANDS_N, MERIDIAN_SLOTS), ((1, 2), (2, 2), (3, 4)), -0.2, 0.2)), 0.05, 5.0)
    face_transport_numbers = jnp.clip(jax.random.uniform(key_list[1], (2, ALTITUDE_TIERS, PARALLEL_BANDS_N, MERIDIAN_SLOTS), jnp.float32, -0.15, 0.15) * block_levels(key_list[1], (2, ALTITUDE_TIERS, PARALLEL_BANDS_N, MERIDIAN_SLOTS), ((1, 2), (2, 2), (3, 4)), -0.4, 0.0), -0.15, 0.15)
    spreading_number = jnp.clip(jnp.exp(jax.random.uniform(key_list[2], (G, ALTITUDE_TIERS), jnp.float32, math.log(0.01), math.log(0.03))), 0.01, 0.03)
    particle_fall_category = set_ends(jax.random.randint(key_list[3], (G,), 0, NCLASS), jax.random.fold_in(key_list[3], 1), 0, NCLASS - 1).astype(jnp.int32)
    crater_parallel_position = set_ends(jax.random.randint(own_keys[4], (NSRC,), 0, PARALLEL_BANDS_N), jax.random.fold_in(own_keys[4], 1), 0, PARALLEL_BANDS_N - 1).astype(jnp.int32)
    crater_meridian_position = set_ends(jax.random.randint(own_keys[5], (NSRC,), 0, MERIDIAN_SLOTS), jax.random.fold_in(own_keys[5], 1), 0, MERIDIAN_SLOTS - 1).astype(jnp.int32)
    crater_release_altitude = set_ends(jax.random.randint(own_keys[6], (NSRC,), 0, ALTITUDE_TIERS), jax.random.fold_in(own_keys[6], 1), 0, ALTITUDE_TIERS - 1).astype(jnp.int32)
    eruption_source_amount = jnp.clip(jnp.exp(jax.random.uniform(own_keys[7], (NSRC, G), jnp.float32, math.log(0.5), math.log(4.0))), 0.5, 4.0)
    optical_depth_factor = jnp.clip(jnp.exp(jax.random.uniform(key_list[8], (NB, G), jnp.float32, math.log(0.005), math.log(0.05))), 0.005, 0.05)
    spectral_radiance_share = jnp.clip(jnp.exp(jax.random.uniform(key_list[9], (NB,), jnp.float32, math.log(0.5), math.log(2.0))), 0.5, 2.0)
    atmosphere_warmth = jnp.clip(200.0 + 90.0 * jax.random.uniform(key_list[10], (ALTITUDE_TIERS, PARALLEL_BANDS_N, MERIDIAN_SLOTS), jnp.float32) ** block_levels(key_list[10], (ALTITUDE_TIERS, PARALLEL_BANDS_N, MERIDIAN_SLOTS), ((0, 2), (1, 2), (2, 4)), -0.2, 0.2), 200.0, 290.0)
    ground_warmth_kelvin = jnp.clip(250.0 + 60.0 * jax.random.uniform(key_list[11], (PARALLEL_BANDS_N, MERIDIAN_SLOTS), jnp.float32) ** block_levels(key_list[11], (PARALLEL_BANDS_N, MERIDIAN_SLOTS), ((0, 2), (1, 4)), -0.2, 0.2), 250.0, 310.0)
    return {"ash_density_field": ash_density_field, "face_transport_numbers": face_transport_numbers, "spreading_number": spreading_number, "particle_fall_category": particle_fall_category, "crater_parallel_position": crater_parallel_position, "crater_meridian_position": crater_meridian_position, "crater_release_altitude": crater_release_altitude, "eruption_source_amount": eruption_source_amount, "optical_depth_factor": optical_depth_factor, "spectral_radiance_share": spectral_radiance_share, "atmosphere_warmth": atmosphere_warmth, "ground_warmth_kelvin": ground_warmth_kelvin}


def update(density, east_cell, west_cell, north_cell, south_cell, above_cell, winds, mixing, settle):
    u_east, u_west, v_north, v_south = winds
    flux_east = jnp.maximum(u_east, 0.0) * density + jnp.minimum(u_east, 0.0) * east_cell
    flux_west = jnp.maximum(u_west, 0.0) * west_cell + jnp.minimum(u_west, 0.0) * density
    flux_north = jnp.maximum(v_north, 0.0) * density + jnp.minimum(v_north, 0.0) * north_cell
    flux_south = jnp.maximum(v_south, 0.0) * south_cell + jnp.minimum(v_south, 0.0) * density
    laplace = east_cell + west_cell + north_cell + south_cell - 4.0 * density
    return density - (flux_east - flux_west) - (flux_north - flux_south) + mixing * laplace + settle * (above_cell - density)


def reference(ash_density_field, face_transport_numbers, spreading_number, particle_fall_category, crater_parallel_position, crater_meridian_position, crater_release_altitude, eruption_source_amount, optical_depth_factor, spectral_radiance_share, atmosphere_warmth, ground_warmth_kelvin):
    u_east = face_transport_numbers[0]
    v_north = face_transport_numbers[1].at[:, PARALLEL_BANDS_N - 1, :].set(0.0)
    u_west = jnp.roll(u_east, 1, axis=2)
    v_south = jnp.concatenate([jnp.zeros_like(v_north[:, :1]), v_north[:, :-1]], axis=1)
    winds = (u_east, u_west, v_north, v_south)
    fall_rate = 0.04 * (1.0 + particle_fall_category.astype(jnp.float32))

    def advance(inputs):
        density, mixing, settle = inputs
        east_cell = jnp.roll(density, -1, axis=2)
        west_cell = jnp.roll(density, 1, axis=2)
        partner = jnp.roll(density, MERIDIAN_SLOTS // 2, axis=2)
        north_cell = jnp.concatenate([density[:, 1:], partner[:, -1:]], axis=1)
        south_cell = jnp.concatenate([partner[:, :1], density[:, :-1]], axis=1)
        above_cell = jnp.concatenate([density[1:], jnp.zeros_like(density[:1])], axis=0)
        return update(density, east_cell, west_cell, north_cell, south_cell, above_cell, winds, mixing[:, None, None], settle)

    density = ash_density_field
    for step_index in range(STEPS):
        density = lax.map(advance, (density, spreading_number, fall_rate))
        density = density.at[:, crater_release_altitude, crater_parallel_position, crater_meridian_position].add(eruption_source_amount.T)

    scale = spectral_radiance_share[:, None, None]
    proportion_quotient = ground_warmth_kelvin / 250.0
    squared = proportion_quotient * proportion_quotient
    radiance = scale * (squared * squared)
    layers = []
    for altitude_tier_position in range(ALTITUDE_TIERS):
        optical = jnp.einsum("bg,gji->bji", optical_depth_factor, density[:, altitude_tier_position], precision=lax.Precision.HIGHEST)
        transmit = jnp.exp(-optical)
        proportion_quotient = atmosphere_warmth[altitude_tier_position] / 250.0
        squared = proportion_quotient * proportion_quotient
        emitted = scale * (squared * squared)
        radiance = radiance * transmit + emitted * (1.0 - transmit)
        layers.append(radiance)
    return density, jnp.stack(layers, axis=1)
```

```python
import functools

import jax
import jax.numpy as jnp
from jax import lax
from jax.experimental import pallas as pl
from jax.experimental.pallas import tpu as pltpu
from jax.sharding import PartitionSpec as P

MESH = pl.DeviceIdType.MESH
STEPS = 2
PAD = 8
CHUNK = 32
F32 = jnp.float32


def kernel(
    sizes,
    ash,
    face,
    air,
    ground,
    spread,
    category,
    vent_row,
    vent_col,
    vent_lev,
    amount,
    depth,
    share,
    settled,
    upward,
    dens_a,
    dens_b,
    vpad,
    coef,
    trans,
    lower_rad,
    sent_rad,
    col_send,
    col_recv,
    col_mix,
    row_send,
    row_recv,
    vent_amount,
    load_sem,
    send_sem,
    recv_sem,
    above_send,
    above_recv,
    rad_send,
    rad_recv,
):
    lon_n, lat_n = sizes
    grains, levels, rows, cols = ash.shape
    bands = depth.shape[0]
    vents = amount.shape[0]
    chunks = rows // CHUNK
    tiles = rows // 8
    lon = lax.axis_index("lon")
    lat = lax.axis_index("lat")
    lev = lax.axis_index("lev")
    is_south = lat == 0
    is_north = lat == lat_n - 1
    east_id = lax.rem(lon + 1, lon_n)
    west_id = lax.rem(lon + lon_n - 1, lon_n)
    partner = lax.rem(lon + lon_n // 2, lon_n)
    north_dev = {
        "lon": jnp.where(is_north, partner, lon),
        "lat": jnp.where(is_north, lat, lat + 1),
    }
    south_dev = {
        "lon": jnp.where(is_south, partner, lon),
        "lat": jnp.where(is_south, lat, lat - 1),
    }
    north_slot = jnp.where(is_north, 1, 0)
    south_slot = jnp.where(is_south, 0, 1)

    loads = []
    for l in range(levels):
        loads.append(
            pltpu.make_async_copy(
                ash.at[:, l], dens_a.at[pl.ds(grains * l, grains), pl.ds(PAD, rows)], load_sem.at[l]
            )
        )
    loads.append(
        pltpu.make_async_copy(face.at[1], vpad.at[:, pl.ds(PAD, rows)], load_sem.at[levels])
    )
    for copy in loads:
        copy.start()

    barrier = pltpu.get_barrier_semaphore()
    for dev in ({"lon": east_id}, {"lon": west_id}, north_dev, south_dev, {"lev": 1 - lev}):
        pl.semaphore_signal(barrier, inc=1, device_id=dev, device_id_type=MESH)

    ids = []
    for s in range(vents):
        r = vent_row[s] - lat * rows
        c = vent_col[s] - lon * cols
        k = vent_lev[s] - lev * levels
        inside = (r >= 0) & (r < rows) & (c >= 0) & (c < cols) & (k >= 0) & (k < levels)
        ids.append(jnp.where(inside, (k * rows + r) * cols + c, -1))
    for s in range(vents):
        for g in range(grains):
            total = amount[s, g]
            for o in range(vents):
                if o != s:
                    total = total + jnp.where(ids[o] == ids[s], amount[o, g], 0.0)
            vent_amount[s, g] = total

    lane = lax.broadcasted_iota(jnp.int32, (CHUNK, cols), 1)
    first_lane = lane == 0
    last_lane = lane == cols - 1
    lane8 = lax.broadcasted_iota(jnp.int32, (8, cols), 1)
    pair8 = lane8 // 2
    even8 = lax.rem(lane8, 2) == 0
    cell = lax.broadcasted_iota(jnp.int32, (CHUNK, cols), 0) * cols + lane

    @pl.when(lev == 1)
    def _():
        zero = jnp.zeros((rows, cols), F32)
        for g in range(grains):
            dens_a[levels * grains + g, pl.ds(PAD, rows), :] = zero
            dens_b[levels * grains + g, pl.ds(PAD, rows), :] = zero

    def pack(step, l, src):
        def turn(t, carry):
            p0, p1 = carry
            at = pl.ds(pl.multiple_of(PAD + 8 * t, 8), 8)
            for q in range(3):
                here = pair8 == 16 * q + t
                move = 32 * q + 2 * t + 1
                p0 = jnp.where(here, pltpu.roll(src[grains * l + 2 * q, at, :], move, 1), p0)
                p1 = jnp.where(here, pltpu.roll(src[grains * l + 2 * q + 1, at, :], move, 1), p1)
            if step == 0:
                here = pair8 == 48 + t
                u = face[0, l, pl.ds(pl.multiple_of(8 * t, 8), 8), :]
                p0 = jnp.where(here, pltpu.roll(u, 97 + 2 * t, 1), p0)
            return p0, p1

        zero = jnp.zeros((8, cols), F32)
        p0, p1 = lax.fori_loop(0, tiles, turn, (zero, zero), unroll=4)
        col_send[step, l, 0] = p0
        col_send[step, l, 1] = p1
        for g in range(grains):
            row_send[step, l, 0, g : g + 1, :] = src[grains * l + g, PAD : PAD + 1, :]
            row_send[step, l, 1, g : g + 1, :] = src[
                grains * l + g, PAD + rows - 1 : PAD + rows, :
            ]
        if step == 0:
            row_send[step, l, 1, grains : grains + 1, :] = vpad[
                l, PAD + rows - 1 : PAD + rows, :
            ]

    def edge_copies(step, l):
        def col(slot, dev):
            return pltpu.make_async_remote_copy(
                src_ref=col_send.at[step, l],
                dst_ref=col_recv.at[step, l, slot],
                send_sem=send_sem.at[step, l, slot],
                recv_sem=recv_sem.at[step, l, slot],
                device_id={"lon": dev},
                device_id_type=MESH,
            )

        def row(edge, slot, dev):
            return pltpu.make_async_remote_copy(
                src_ref=row_send.at[step, l, edge],
                dst_ref=row_recv.at[step, l, slot],
                send_sem=send_sem.at[step, l, 2 + edge],
                recv_sem=recv_sem.at[step, l, 2 + slot],
                device_id=dev,
                device_id_type=MESH,
            )

        return [
            col(0, east_id),
            col(1, west_id),
            row(0, south_slot, south_dev),
            row(1, north_slot, north_dev),
        ]

    def wait_edges(step, l, src):
        for slot in range(2):
            pltpu.make_async_remote_copy(
                src_ref=col_send.at[step, l],
                dst_ref=col_recv.at[step, l, slot],
                send_sem=send_sem.at[step, l, slot],
                recv_sem=recv_sem.at[step, l, slot],
                device_id={"lon": east_id},
                device_id_type=MESH,
            ).wait_recv()
            pltpu.make_async_remote_copy(
                src_ref=row_send.at[step, l, slot],
                dst_ref=row_recv.at[step, l, slot],
                send_sem=send_sem.at[step, l, 2 + slot],
                recv_sem=recv_sem.at[step, l, 2 + slot],
                device_id={"lon": east_id},
                device_id_type=MESH,
            ).wait_recv()
        for v in range(2):
            col_mix[step, l, v] = jnp.where(
                even8, col_recv[step, l, 0, v], col_recv[step, l, 1, v]
            )
        for g in range(grains):
            src[grains * l + g, PAD - 1 : PAD, :] = row_recv[step, l, 0, g : g + 1, :]
            src[grains * l + g, PAD + rows : PAD + rows + 1, :] = row_recv[
                step, l, 1, g : g + 1, :
            ]
        if step == 0:
            row = row_recv[step, l, 0, grains : grains + 1, :]
            vpad[l, PAD - 1 : PAD, :] = jnp.where(is_south, jnp.zeros_like(row), row)

    def halo_lanes(packed, slot, c):
        parts = []
        for j in range(CHUNK // 8):
            t = c * (CHUNK // 8) + j
            parts.append(pltpu.roll(packed, cols - (32 * (slot // 2) + 2 * t + 1), 1))
        return jnp.concatenate(parts, axis=0)

    def advance(step, l, c, src, store):
        base = pl.multiple_of(c * CHUNK, CHUNK)
        mid = pl.ds(PAD + base, CHUNK)
        mix = [col_mix[step, l, v] for v in range(2)]
        plain = pl.ds(base, CHUNK)
        if step == 0:
            ue = face[0, l, plain, :]
            uw = pltpu.roll(jnp.where(last_lane, halo_lanes(mix[0], 6, c), ue), 1, 1)
            vn = vpad[l, mid, :]
            vs = vpad[l, pl.ds(PAD - 1 + base, CHUNK), :]
            pe, pw = -jnp.minimum(ue, 0.0), jnp.maximum(uw, 0.0)
            pn, ps = -jnp.minimum(vn, 0.0), jnp.maximum(vs, 0.0)
            own = (
                1.0
                - jnp.maximum(ue, 0.0)
                + jnp.minimum(uw, 0.0)
                - jnp.maximum(vn, 0.0)
                + jnp.minimum(vs, 0.0)
            )
            for j, value in enumerate((pe, pw, pn, ps, own)):
                coef[l, j, plain, :] = value
        else:
            pe, pw, pn, ps, own = (coef[l, j, plain, :] for j in range(5))
        offset = (l * rows + base) * cols
        hits = [cell == ids[s] - offset for s in range(vents)]
        for g in range(grains):
            i = grains * l + g
            x = src[i, mid, :]
            south = src[i, pl.ds(PAD - 1 + base, CHUNK), :]
            north = src[i, pl.ds(PAD + 1 + base, CHUNK), :]
            above = src[i + grains, mid, :]
            edge = halo_lanes(mix[g % 2], g, c)
            west = pltpu.roll(jnp.where(last_lane, edge, x), 1, 1)
            east = pltpu.roll(jnp.where(first_lane, edge, x), cols - 1, 1)
            m = spread[g, lev * levels + l]
            f = 0.04 * (1.0 + category[g].astype(F32))
            new = (
                (own - (4.0 * m + f)) * x
                + (pe + m) * east
                + (pw + m) * west
                + (pn + m) * north
                + (ps + m) * south
                + f * above
            )
            erupt = jnp.zeros_like(new)
            for s in range(vents):
                erupt = jnp.where(hits[s], vent_amount[s, g], erupt)
            store(g, mid, plain, new + erupt)

    def above_copy(step, src):
        return pltpu.make_async_remote_copy(
            src_ref=src.at[pl.ds(0, grains), pl.ds(PAD, rows)],
            dst_ref=src.at[pl.ds(levels * grains, grains), pl.ds(PAD, rows)],
            send_sem=above_send.at[step],
            recv_sem=above_recv.at[step],
            device_id={"lev": 1 - lev},
            device_id_type=MESH,
        )

    def rad_copy(c):
        part = pl.ds(pl.multiple_of(c * CHUNK, CHUNK), CHUNK)
        return pltpu.make_async_remote_copy(
            src_ref=sent_rad.at[:, part],
            dst_ref=lower_rad.at[:, part],
            send_sem=rad_send.at[c],
            recv_sem=rad_recv.at[c],
            device_id={"lev": 1 - lev},
            device_id_type=MESH,
        )

    for copy in loads:
        copy.wait()

    @pl.when(is_north)
    def _():
        for l in range(levels):
            vpad[l, PAD + rows - 1 : PAD + rows, :] = jnp.zeros((1, cols), F32)

    pack(0, 0, dens_a)
    pl.semaphore_wait(barrier, 5)
    for copy in edge_copies(0, 0):
        copy.start()

    @pl.when(lev == 1)
    def _():
        above_copy(0, dens_a).start()

    pack(0, 1, dens_a)
    for copy in edge_copies(0, 1):
        copy.start()

    def loop(body):
        def turn(c, carry):
            body(c)
            return carry

        lax.fori_loop(0, chunks, turn, 0)

    for l in range(levels):
        wait_edges(0, l, dens_a)
        if l == levels - 1:

            @pl.when(lev == 0)
            def _():
                above_copy(0, dens_a).wait_recv()

        def store(g, mid, plain, value, l=l):
            dens_b[grains * l + g, mid, :] = value

        loop(lambda c: advance(0, l, c, dens_a, store))
        pack(1, l, dens_b)
        for copy in edge_copies(1, l):
            copy.start()
        if l == 0:

            @pl.when(lev == 1)
            def _():
                above_copy(1, dens_b).start()

    def fourth(value):
        ratio = value / 250.0
        squared = ratio * ratio
        return squared * squared

    def finish(c, below):
        plain = pl.ds(pl.multiple_of(c * CHUNK, CHUNK), CHUNK)
        warm = [fourth(air[l, plain, :]) for l in range(levels)]
        for b in range(bands):
            rad = below(b, plain)
            for l in range(levels):
                rad = warm[l] + trans[b, l, plain, :] * (rad - warm[l])
                upward[b, l, plain, :] = share[b] * rad
            sent_rad[b, plain, :] = rad

    for l in range(levels):
        wait_edges(1, l, dens_b)
        if l == levels - 1:

            @pl.when(lev == 0)
            def _():
                above_copy(1, dens_b).wait_recv()

        def store(g, mid, plain, value, l=l):
            settled[g, l, plain, :] = value

        def second(c, l=l):
            advance(1, l, c, dens_b, store)
            plain = pl.ds(pl.multiple_of(c * CHUNK, CHUNK), CHUNK)
            field = [settled[g, l, plain, :] for g in range(grains)]
            for b in range(bands):
                optical = depth[b, 0] * field[0]
                for g in range(1, grains):
                    optical = optical + depth[b, g] * field[g]
                trans[b, l, plain, :] = jnp.exp(-optical)
            if l == levels - 1:

                @pl.when(lev == 0)
                def _():
                    heat = fourth(ground[plain, :])
                    finish(c, lambda b, part: heat)
                    rad_copy(c).start()

        loop(second)

    @pl.when(lev == 1)
    def _():
        def last(c):
            rad_copy(c).wait_recv()
            finish(c, lambda b, part: lower_rad[b, part, :])

        loop(last)

    for step in range(STEPS):
        for l in range(levels):
            for copy in edge_copies(step, l):
                copy.wait_send()

    @pl.when(lev == 1)
    def _():
        above_copy(0, dens_a).wait_send()
        above_copy(1, dens_b).wait_send()

    @pl.when(lev == 0)
    def _():
        loop(lambda c: rad_copy(c).wait_send())


def per_device(sizes, *args):
    (ash, face, spread, category, vrow, vcol, vlev, amount, depth, share, air, ground) = args
    grains, levels, rows, cols = ash.shape
    bands = depth.shape[0]
    vmem = pl.BlockSpec(memory_space=pltpu.VMEM)
    smem = pl.BlockSpec(memory_space=pltpu.SMEM)
    slots = (levels + 1) * grains
    scratch = [
        pltpu.VMEM((slots, rows + 2 * PAD, cols), F32),
        pltpu.VMEM((slots, rows + 2 * PAD, cols), F32),
        pltpu.VMEM((levels, rows + 2 * PAD, cols), F32),
        pltpu.VMEM((levels, 5, rows, cols), F32),
        pltpu.VMEM((bands, levels, rows, cols), F32),
        pltpu.VMEM((bands, rows, cols), F32),
        pltpu.VMEM((bands, rows, cols), F32),
        pltpu.VMEM((STEPS, levels, 2, 8, cols), F32),
        pltpu.VMEM((STEPS, levels, 2, 2, 8, cols), F32),
        pltpu.VMEM((STEPS, levels, 2, 8, cols), F32),
        pltpu.VMEM((STEPS, levels, 2, 8, cols), F32),
        pltpu.VMEM((STEPS, levels, 2, 8, cols), F32),
        pltpu.SMEM(amount.shape, F32),
        pltpu.SemaphoreType.DMA((levels + 1,)),
        pltpu.SemaphoreType.DMA((STEPS, levels, 4)),
        pltpu.SemaphoreType.DMA((STEPS, levels, 4)),
        pltpu.SemaphoreType.DMA((STEPS,)),
        pltpu.SemaphoreType.DMA((STEPS,)),
        pltpu.SemaphoreType.DMA((rows // CHUNK,)),
        pltpu.SemaphoreType.DMA((rows // CHUNK,)),
    ]
    return pl.pallas_call(
        functools.partial(kernel, sizes),
        out_shape=(
            jax.ShapeDtypeStruct(ash.shape, F32),
            jax.ShapeDtypeStruct((bands, levels, rows, cols), F32),
        ),
        in_specs=[vmem] * 4 + [smem] * 8,
        out_specs=(vmem, vmem),
        scratch_shapes=scratch,
        compiler_params=pltpu.CompilerParams(
            collective_id=0, has_side_effects=True, vmem_limit_bytes=32 * 1024 * 1024
        ),
    )(ash, face, air, ground, spread, category, vrow, vcol, vlev, amount, depth, share)


def solution(mesh):
    sizes = (mesh.shape["lon"], mesh.shape["lat"])
    field = P("members", "lev", "lat", "lon")
    placed = (
        field,
        P(None, "lev", "lat", "lon"),
        P(),
        P(),
        P("members"),
        P("members"),
        P("members"),
        P("members", None),
        P(),
        P(),
        P("lev", "lat", "lon"),
        P("lat", "lon"),
    )
    return jax.shard_map(
        functools.partial(per_device, sizes),
        mesh=mesh,
        in_specs=placed,
        out_specs=(field, field),
        check_vma=False,
    )
```

```python
import functools

import jax
import jax.numpy as jnp
from jax import lax
from jax.experimental import pallas as pl
from jax.experimental.pallas import tpu as pltpu
from jax.sharding import PartitionSpec as P

MESH = pl.DeviceIdType.MESH
STEPS = 2
PAD = 8
CHUNK = 32
F32 = jnp.float32


def kernel(
    sizes,
    ash,
    face_hbm,
    air_hbm,
    ground_hbm,
    *rest,
):
    smalls, rest = rest[:8], rest[8:]
    small_copies, rest = rest[-9:-1], rest[:-9] + rest[-1:]
    body(sizes, ash, face_hbm, air_hbm, ground_hbm, smalls, *small_copies, *rest)


def body(
    sizes,
    ash,
    face_hbm,
    air_hbm,
    ground_hbm,
    smalls,
    spread,
    category,
    vent_row,
    vent_col,
    vent_lev,
    amount,
    depth,
    share,
    settled,
    upward,
    face,
    air,
    ground,
    dens_a,
    dens_b,
    vpad,
    coef,
    trans,
    lower_rad,
    sent_rad,
    col_send,
    col_recv,
    col_mix,
    row_send,
    row_recv,
    vent_amount,
    load_sem,
    send_sem,
    recv_sem,
    above_send,
    above_recv,
    rad_send,
    rad_recv,
    small_sem,
):
    lon_n, lat_n = sizes
    grains, levels, rows, cols = ash.shape
    bands = depth.shape[0]
    vents = amount.shape[0]
    chunks = rows // CHUNK
    tiles = rows // 8
    lon = lax.axis_index("lon")
    lat = lax.axis_index("lat")
    lev = lax.axis_index("lev")
    is_south = lat == 0
    is_north = lat == lat_n - 1
    east_id = lax.rem(lon + 1, lon_n)
    west_id = lax.rem(lon + lon_n - 1, lon_n)
    partner = lax.rem(lon + lon_n // 2, lon_n)
    north_dev = {
        "lon": jnp.where(is_north, partner, lon),
        "lat": jnp.where(is_north, lat, lat + 1),
    }
    south_dev = {
        "lon": jnp.where(is_south, partner, lon),
        "lat": jnp.where(is_south, lat, lat - 1),
    }
    north_slot = jnp.where(is_north, 1, 0)
    south_slot = jnp.where(is_south, 0, 1)

    loads = []
    for l in range(levels):
        loads.append(
            pltpu.make_async_copy(
                ash.at[:, l], dens_a.at[pl.ds(grains * l, grains), pl.ds(PAD, rows)], load_sem.at[l]
            )
        )
    loads.append(
        pltpu.make_async_copy(face_hbm.at[1], vpad.at[:, pl.ds(PAD, rows)], load_sem.at[levels])
    )
    loads.append(pltpu.make_async_copy(face_hbm.at[0], face, load_sem.at[levels + 1]))
    late = [
        pltpu.make_async_copy(air_hbm, air, load_sem.at[levels + 2]),
        pltpu.make_async_copy(ground_hbm, ground, load_sem.at[levels + 3]),
    ]
    held = (spread, category, vent_row, vent_col, vent_lev, amount, depth, share)
    little = [
        pltpu.make_async_copy(source, target, small_sem.at[n])
        for n, (source, target) in enumerate(zip(smalls, held))
    ]
    for copy in loads + little + late:
        copy.start()

    barrier = pltpu.get_barrier_semaphore()
    for dev in ({"lon": east_id}, {"lon": west_id}, north_dev, south_dev, {"lev": 1 - lev}):
        pl.semaphore_signal(barrier, inc=1, device_id=dev, device_id_type=MESH)

    for copy in little:
        copy.wait()

    ids = []
    for s in range(vents):
        r = vent_row[s] - lat * rows
        c = vent_col[s] - lon * cols
        k = vent_lev[s] - lev * levels
        inside = (r >= 0) & (r < rows) & (c >= 0) & (c < cols) & (k >= 0) & (k < levels)
        ids.append(jnp.where(inside, (k * rows + r) * cols + c, -1))
    for s in range(vents):
        for g in range(grains):
            total = amount[s, g]
            for o in range(vents):
                if o != s:
                    total = total + jnp.where(ids[o] == ids[s], amount[o, g], 0.0)
            vent_amount[s, g] = total

    lane = lax.broadcasted_iota(jnp.int32, (CHUNK, cols), 1)
    first_lane = lane == 0
    last_lane = lane == cols - 1
    lane8 = lax.broadcasted_iota(jnp.int32, (8, cols), 1)
    pair8 = lane8 // 2
    even8 = lax.rem(lane8, 2) == 0
    cell = lax.broadcasted_iota(jnp.int32, (CHUNK, cols), 0) * cols + lane

    @pl.when(lev == 1)
    def _():
        zero = jnp.zeros((rows, cols), F32)
        for g in range(grains):
            dens_a[levels * grains + g, pl.ds(PAD, rows), :] = zero
            dens_b[levels * grains + g, pl.ds(PAD, rows), :] = zero

    def pack(step, l, src):
        def turn(t, carry):
            p0, p1 = carry
            at = pl.ds(pl.multiple_of(PAD + 8 * t, 8), 8)
            for q in range(3):
                here = pair8 == 16 * q + t
                move = 32 * q + 2 * t + 1
                p0 = jnp.where(here, pltpu.roll(src[grains * l + 2 * q, at, :], move, 1), p0)
                p1 = jnp.where(here, pltpu.roll(src[grains * l + 2 * q + 1, at, :], move, 1), p1)
            if step == 0:
                here = pair8 == 48 + t
                u = face[l, pl.ds(pl.multiple_of(8 * t, 8), 8), :]
                p0 = jnp.where(here, pltpu.roll(u, 97 + 2 * t, 1), p0)
            return p0, p1

        zero = jnp.zeros((8, cols), F32)
        p0, p1 = lax.fori_loop(0, tiles, turn, (zero, zero), unroll=4)
        col_send[step, l, 0] = p0
        col_send[step, l, 1] = p1
        for g in range(grains):
            row_send[step, l, 0, g : g + 1, :] = src[grains * l + g, PAD : PAD + 1, :]
            row_send[step, l, 1, g : g + 1, :] = src[
                grains * l + g, PAD + rows - 1 : PAD + rows, :
            ]
        if step == 0:
            row_send[step, l, 1, grains : grains + 1, :] = vpad[
                l, PAD + rows - 1 : PAD + rows, :
            ]

    def edge_copies(step, l):
        def col(slot, dev):
            return pltpu.make_async_remote_copy(
                src_ref=col_send.at[step, l],
                dst_ref=col_recv.at[step, l, slot],
                send_sem=send_sem.at[step, l, slot],
                recv_sem=recv_sem.at[step, l, slot],
                device_id={"lon": dev},
                device_id_type=MESH,
            )

        def row(edge, slot, dev):
            return pltpu.make_async_remote_copy(
                src_ref=row_send.at[step, l, edge],
                dst_ref=row_recv.at[step, l, slot],
                send_sem=send_sem.at[step, l, 2 + edge],
                recv_sem=recv_sem.at[step, l, 2 + slot],
                device_id=dev,
                device_id_type=MESH,
            )

        return [
            col(0, east_id),
            col(1, west_id),
            row(0, south_slot, south_dev),
            row(1, north_slot, north_dev),
        ]

    def wait_edges(step, l, src):
        for slot in range(2):
            pltpu.make_async_remote_copy(
                src_ref=col_send.at[step, l],
                dst_ref=col_recv.at[step, l, slot],
                send_sem=send_sem.at[step, l, slot],
                recv_sem=recv_sem.at[step, l, slot],
                device_id={"lon": east_id},
                device_id_type=MESH,
            ).wait_recv()
            pltpu.make_async_remote_copy(
                src_ref=row_send.at[step, l, slot],
                dst_ref=row_recv.at[step, l, slot],
                send_sem=send_sem.at[step, l, 2 + slot],
                recv_sem=recv_sem.at[step, l, 2 + slot],
                device_id={"lon": east_id},
                device_id_type=MESH,
            ).wait_recv()
        for v in range(2):
            col_mix[step, l, v] = jnp.where(
                even8, col_recv[step, l, 0, v], col_recv[step, l, 1, v]
            )
        for g in range(grains):
            src[grains * l + g, PAD - 1 : PAD, :] = row_recv[step, l, 0, g : g + 1, :]
            src[grains * l + g, PAD + rows : PAD + rows + 1, :] = row_recv[
                step, l, 1, g : g + 1, :
            ]
        if step == 0:
            row = row_recv[step, l, 0, grains : grains + 1, :]
            vpad[l, PAD - 1 : PAD, :] = jnp.where(is_south, jnp.zeros_like(row), row)

    def halo_lanes(packed, slot, c):
        parts = []
        for j in range(CHUNK // 8):
            t = c * (CHUNK // 8) + j
            parts.append(pltpu.roll(packed, cols - (32 * (slot // 2) + 2 * t + 1), 1))
        return jnp.concatenate(parts, axis=0)

    def advance(step, l, c, src, store):
        base = pl.multiple_of(c * CHUNK, CHUNK)
        mid = pl.ds(PAD + base, CHUNK)
        mix = [col_mix[step, l, v] for v in range(2)]
        plain = pl.ds(base, CHUNK)
        if step == 0:
            ue = face[l, plain, :]
            uw = pltpu.roll(jnp.where(last_lane, halo_lanes(mix[0], 6, c), ue), 1, 1)
            vn = vpad[l, mid, :]
            vs = vpad[l, pl.ds(PAD - 1 + base, CHUNK), :]
            pe, pw = -jnp.minimum(ue, 0.0), jnp.maximum(uw, 0.0)
            pn, ps = -jnp.minimum(vn, 0.0), jnp.maximum(vs, 0.0)
            own = (
                1.0
                - jnp.maximum(ue, 0.0)
                + jnp.minimum(uw, 0.0)
                - jnp.maximum(vn, 0.0)
                + jnp.minimum(vs, 0.0)
            )
            for j, value in enumerate((pe, pw, pn, ps, own)):
                coef[l, j, plain, :] = value
        else:
            pe, pw, pn, ps, own = (coef[l, j, plain, :] for j in range(5))
        offset = (l * rows + base) * cols
        hits = [cell == ids[s] - offset for s in range(vents)]
        for g in range(grains):
            i = grains * l + g
            x = src[i, mid, :]
            south = src[i, pl.ds(PAD - 1 + base, CHUNK), :]
            north = src[i, pl.ds(PAD + 1 + base, CHUNK), :]
            above = src[i + grains, mid, :]
            edge = halo_lanes(mix[g % 2], g, c)
            west = pltpu.roll(jnp.where(last_lane, edge, x), 1, 1)
            east = pltpu.roll(jnp.where(first_lane, edge, x), cols - 1, 1)
            m = spread[lev * levels + l, g]
            f = 0.04 * (1.0 + category[g].astype(F32))
            new = (
                (own - (4.0 * m + f)) * x
                + (pe + m) * east
                + (pw + m) * west
                + (pn + m) * north
                + (ps + m) * south
                + f * above
            )
            erupt = jnp.zeros_like(new)
            for s in range(vents):
                erupt = jnp.where(hits[s], vent_amount[s, g], erupt)
            store(g, mid, plain, new + erupt)

    def above_copy(step, src):
        return pltpu.make_async_remote_copy(
            src_ref=src.at[pl.ds(0, grains), pl.ds(PAD, rows)],
            dst_ref=src.at[pl.ds(levels * grains, grains), pl.ds(PAD, rows)],
            send_sem=above_send.at[step],
            recv_sem=above_recv.at[step],
            device_id={"lev": 1 - lev},
            device_id_type=MESH,
        )

    def rad_copy(c):
        part = pl.ds(pl.multiple_of(c * CHUNK, CHUNK), CHUNK)
        return pltpu.make_async_remote_copy(
            src_ref=sent_rad.at[:, part],
            dst_ref=lower_rad.at[:, part],
            send_sem=rad_send.at[c],
            recv_sem=rad_recv.at[c],
            device_id={"lev": 1 - lev},
            device_id_type=MESH,
        )

    for copy in loads:
        copy.wait()

    @pl.when(is_north)
    def _():
        for l in range(levels):
            vpad[l, PAD + rows - 1 : PAD + rows, :] = jnp.zeros((1, cols), F32)

    pack(0, 0, dens_a)
    pl.semaphore_wait(barrier, 5)
    for copy in edge_copies(0, 0):
        copy.start()

    @pl.when(lev == 1)
    def _():
        above_copy(0, dens_a).start()

    pack(0, 1, dens_a)
    for copy in edge_copies(0, 1):
        copy.start()

    def loop(body):
        def turn(c, carry):
            body(c)
            return carry

        lax.fori_loop(0, chunks, turn, 0)

    for l in range(levels):
        wait_edges(0, l, dens_a)
        if l == levels - 1:

            @pl.when(lev == 0)
            def _():
                above_copy(0, dens_a).wait_recv()

        def store(g, mid, plain, value, l=l):
            dens_b[grains * l + g, mid, :] = value

        loop(lambda c: advance(0, l, c, dens_a, store))
        pack(1, l, dens_b)
        for copy in edge_copies(1, l):
            copy.start()
        if l == 0:

            @pl.when(lev == 1)
            def _():
                above_copy(1, dens_b).start()

    def fourth(value):
        ratio = value / 250.0
        squared = ratio * ratio
        return squared * squared

    def finish(c, below):
        plain = pl.ds(pl.multiple_of(c * CHUNK, CHUNK), CHUNK)
        warm = [fourth(air[l, plain, :]) for l in range(levels)]
        for b in range(bands):
            rad = below(b, plain)
            for l in range(levels):
                rad = warm[l] + trans[b, l, plain, :] * (rad - warm[l])
                upward[b, l, plain, :] = share[b] * rad
            sent_rad[b, plain, :] = rad

    for copy in late:
        copy.wait()
    for l in range(levels):
        wait_edges(1, l, dens_b)
        if l == levels - 1:

            @pl.when(lev == 0)
            def _():
                above_copy(1, dens_b).wait_recv()

        def store(g, mid, plain, value, l=l):
            settled[g, l, plain, :] = value

        def second(c, l=l):
            advance(1, l, c, dens_b, store)
            plain = pl.ds(pl.multiple_of(c * CHUNK, CHUNK), CHUNK)
            field = [settled[g, l, plain, :] for g in range(grains)]
            for b in range(bands):
                optical = depth[b, 0] * field[0]
                for g in range(1, grains):
                    optical = optical + depth[b, g] * field[g]
                trans[b, l, plain, :] = jnp.exp(-optical)
            if l == levels - 1:

                @pl.when(lev == 0)
                def _():
                    heat = fourth(ground[plain, :])
                    finish(c, lambda b, part: heat)
                    rad_copy(c).start()

        loop(second)

    @pl.when(lev == 1)
    def _():
        def last(c):
            rad_copy(c).wait_recv()
            finish(c, lambda b, part: lower_rad[b, part, :])

        loop(last)

    for step in range(STEPS):
        for l in range(levels):
            for copy in edge_copies(step, l):
                copy.wait_send()

    @pl.when(lev == 1)
    def _():
        above_copy(0, dens_a).wait_send()
        above_copy(1, dens_b).wait_send()

    @pl.when(lev == 0)
    def _():
        loop(lambda c: rad_copy(c).wait_send())


def per_device(sizes, *args):
    (ash, face, spread, category, vrow, vcol, vlev, amount, depth, share, air, ground) = args
    grains, levels, rows, cols = ash.shape
    bands = depth.shape[0]
    vmem = pl.BlockSpec(memory_space=pltpu.VMEM)
    slots = (levels + 1) * grains
    scratch = [
        pltpu.VMEM((levels, rows, cols), F32),
        pltpu.VMEM((levels, rows, cols), F32),
        pltpu.VMEM((rows, cols), F32),
        pltpu.VMEM((slots, rows + 2 * PAD, cols), F32),
        pltpu.VMEM((slots, rows + 2 * PAD, cols), F32),
        pltpu.VMEM((levels, rows + 2 * PAD, cols), F32),
        pltpu.VMEM((levels, 5, rows, cols), F32),
        pltpu.VMEM((bands, levels, rows, cols), F32),
        pltpu.VMEM((bands, rows, cols), F32),
        pltpu.VMEM((bands, rows, cols), F32),
        pltpu.VMEM((STEPS, levels, 2, 8, cols), F32),
        pltpu.VMEM((STEPS, levels, 2, 2, 8, cols), F32),
        pltpu.VMEM((STEPS, levels, 2, 8, cols), F32),
        pltpu.VMEM((STEPS, levels, 2, 8, cols), F32),
        pltpu.VMEM((STEPS, levels, 2, 8, cols), F32),
        pltpu.SMEM(amount.shape, F32),
        pltpu.SemaphoreType.DMA((levels + 4,)),
        pltpu.SemaphoreType.DMA((STEPS, levels, 4)),
        pltpu.SemaphoreType.DMA((STEPS, levels, 4)),
        pltpu.SemaphoreType.DMA((STEPS,)),
        pltpu.SemaphoreType.DMA((STEPS,)),
        pltpu.SemaphoreType.DMA((rows // CHUNK,)),
        pltpu.SemaphoreType.DMA((rows // CHUNK,)),
    ]
    smalls = (spread.T, category, vrow, vcol, vlev, amount, depth, share)
    scratch += [pltpu.SMEM(small.shape, small.dtype) for small in smalls]
    scratch.append(pltpu.SemaphoreType.DMA((len(smalls),)))
    hbm = pl.BlockSpec(memory_space=pltpu.HBM)
    return pl.pallas_call(
        functools.partial(kernel, sizes),
        out_shape=(
            jax.ShapeDtypeStruct(ash.shape, F32),
            jax.ShapeDtypeStruct((bands, levels, rows, cols), F32),
        ),
        in_specs=[hbm] * (4 + len(smalls)),
        out_specs=(vmem, vmem),
        scratch_shapes=scratch,
        compiler_params=pltpu.CompilerParams(
            collective_id=0, has_side_effects=True, vmem_limit_bytes=32 * 1024 * 1024
        ),
    )(*[pltpu.with_memory_space_constraint(x, pltpu.HBM) for x in (ash, face, air, ground, *smalls)])


def solution(mesh):
    sizes = (mesh.shape["lon"], mesh.shape["lat"])
    field = P("members", "lev", "lat", "lon")
    placed = (
        field,
        P(None, "lev", "lat", "lon"),
        P(),
        P(),
        P("members"),
        P("members"),
        P("members"),
        P("members", None),
        P(),
        P(),
        P("lev", "lat", "lon"),
        P("lat", "lon"),
    )
    return jax.shard_map(
        functools.partial(per_device, sizes),
        mesh=mesh,
        in_specs=placed,
        out_specs=(field, field),
        check_vma=False,
    )
```

```python
import functools

import jax
import jax.numpy as jnp
from jax import lax
from jax.experimental import pallas as pl
from jax.experimental.pallas import tpu as pltpu
from jax.sharding import PartitionSpec as P

MESH = pl.DeviceIdType.MESH
STEPS = 2
PAD = 8
CHUNK = 32
F32 = jnp.float32


def kernel(
    sizes,
    ash,
    face_hbm,
    air_hbm,
    ground_hbm,
    *rest,
):
    smalls, rest = rest[:8], rest[8:]
    small_copies, rest = rest[-9:-1], rest[:-9] + rest[-1:]
    body(sizes, ash, face_hbm, air_hbm, ground_hbm, smalls, *small_copies, *rest)


def body(
    sizes,
    ash,
    face_hbm,
    air_hbm,
    ground_hbm,
    smalls,
    spread,
    category,
    vent_row,
    vent_col,
    vent_lev,
    amount,
    depth,
    share,
    settled,
    upward,
    face,
    air,
    ground,
    dens_a,
    dens_b,
    vpad,
    coef,
    trans,
    lower_rad,
    sent_rad,
    col_send,
    col_recv,
    col_mix,
    row_send,
    row_recv,
    vent_amount,
    load_sem,
    send_sem,
    recv_sem,
    above_send,
    above_recv,
    rad_send,
    rad_recv,
    small_sem,
):
    lon_n, lat_n = sizes
    grains, levels, rows, cols = ash.shape
    bands = depth.shape[0]
    vents = amount.shape[0]
    chunks = rows // CHUNK
    tiles = rows // 8
    lon = lax.axis_index("lon")
    lat = lax.axis_index("lat")
    lev = lax.axis_index("lev")
    is_south = lat == 0
    is_north = lat == lat_n - 1
    east_id = lax.rem(lon + 1, lon_n)
    west_id = lax.rem(lon + lon_n - 1, lon_n)
    partner = lax.rem(lon + lon_n // 2, lon_n)
    north_dev = {
        "lon": jnp.where(is_north, partner, lon),
        "lat": jnp.where(is_north, lat, lat + 1),
    }
    south_dev = {
        "lon": jnp.where(is_south, partner, lon),
        "lat": jnp.where(is_south, lat, lat - 1),
    }
    north_slot = jnp.where(is_north, 1, 0)
    south_slot = jnp.where(is_south, 0, 1)

    barrier = pltpu.get_barrier_semaphore()
    for dev in ({"lon": east_id}, {"lon": west_id}, north_dev, south_dev, {"lev": 1 - lev}):
        pl.semaphore_signal(barrier, inc=1, device_id=dev, device_id_type=MESH)

    loads = []
    for l in range(levels):
        loads.append(
            pltpu.make_async_copy(
                ash.at[:, l], dens_a.at[pl.ds(grains * l, grains), pl.ds(PAD, rows)], load_sem.at[l]
            )
        )
    loads.append(
        pltpu.make_async_copy(face_hbm.at[1], vpad.at[:, pl.ds(PAD, rows)], load_sem.at[levels])
    )
    loads.append(pltpu.make_async_copy(face_hbm.at[0], face, load_sem.at[levels + 1]))
    late = [
        pltpu.make_async_copy(air_hbm, air, load_sem.at[levels + 2]),
        pltpu.make_async_copy(ground_hbm, ground, load_sem.at[levels + 3]),
    ]
    held = (spread, category, vent_row, vent_col, vent_lev, amount, depth, share)
    little = [
        pltpu.make_async_copy(source, target, small_sem.at[n])
        for n, (source, target) in enumerate(zip(smalls, held))
    ]
    for copy in loads + little + late:
        copy.start()

    for copy in little:
        copy.wait()

    ids = []
    for s in range(vents):
        r = vent_row[s] - lat * rows
        c = vent_col[s] - lon * cols
        k = vent_lev[s] - lev * levels
        inside = (r >= 0) & (r < rows) & (c >= 0) & (c < cols) & (k >= 0) & (k < levels)
        ids.append(jnp.where(inside, (k * rows + r) * cols + c, -1))
    for s in range(vents):
        for g in range(grains):
            total = amount[s, g]
            for o in range(vents):
                if o != s:
                    total = total + jnp.where(ids[o] == ids[s], amount[o, g], 0.0)
            vent_amount[s, g] = total

    lane = lax.broadcasted_iota(jnp.int32, (CHUNK, cols), 1)
    first_lane = lane == 0
    last_lane = lane == cols - 1
    lane8 = lax.broadcasted_iota(jnp.int32, (8, cols), 1)
    pair8 = lane8 // 2
    even8 = lax.rem(lane8, 2) == 0
    cell = lax.broadcasted_iota(jnp.int32, (CHUNK, cols), 0) * cols + lane

    no_row = jnp.zeros((1, cols), F32)
    for l in range(levels):
        vpad[l, PAD - 1 : PAD, :] = no_row
        for g in range(grains):
            for dens in (dens_a, dens_b):
                dens[grains * l + g, PAD - 1 : PAD, :] = no_row
                dens[grains * l + g, PAD + rows : PAD + rows + 1, :] = no_row

    @pl.when(lev == 1)
    def _():
        zero = jnp.zeros((rows, cols), F32)
        for g in range(grains):
            dens_a[levels * grains + g, pl.ds(PAD, rows), :] = zero
            dens_b[levels * grains + g, pl.ds(PAD, rows), :] = zero

    def pack(step, l, src):
        def turn(t, carry):
            p0, p1 = carry
            at = pl.ds(pl.multiple_of(PAD + 8 * t, 8), 8)
            for q in range(3):
                here = pair8 == 16 * q + t
                move = 32 * q + 2 * t + 1
                p0 = jnp.where(here, pltpu.roll(src[grains * l + 2 * q, at, :], move, 1), p0)
                p1 = jnp.where(here, pltpu.roll(src[grains * l + 2 * q + 1, at, :], move, 1), p1)
            if step == 0:
                here = pair8 == 48 + t
                u = face[l, pl.ds(pl.multiple_of(8 * t, 8), 8), :]
                p0 = jnp.where(here, pltpu.roll(u, 97 + 2 * t, 1), p0)
            return p0, p1

        zero = jnp.zeros((8, cols), F32)
        p0, p1 = lax.fori_loop(0, tiles, turn, (zero, zero), unroll=4)
        col_send[step, l, 0] = p0
        col_send[step, l, 1] = p1
        for g in range(grains):
            row_send[step, l, 0, g : g + 1, :] = src[grains * l + g, PAD : PAD + 1, :]
            row_send[step, l, 1, g : g + 1, :] = src[
                grains * l + g, PAD + rows - 1 : PAD + rows, :
            ]
        if step == 0:
            row_send[step, l, 1, grains : grains + 1, :] = vpad[
                l, PAD + rows - 1 : PAD + rows, :
            ]

    def edge_copies(step, l):
        def col(slot, dev):
            return pltpu.make_async_remote_copy(
                src_ref=col_send.at[step, l],
                dst_ref=col_recv.at[step, l, slot],
                send_sem=send_sem.at[step, l, slot],
                recv_sem=recv_sem.at[step, l, slot],
                device_id={"lon": dev},
                device_id_type=MESH,
            )

        def row(edge, slot, dev):
            return pltpu.make_async_remote_copy(
                src_ref=row_send.at[step, l, edge],
                dst_ref=row_recv.at[step, l, slot],
                send_sem=send_sem.at[step, l, 2 + edge],
                recv_sem=recv_sem.at[step, l, 2 + slot],
                device_id=dev,
                device_id_type=MESH,
            )

        return [
            col(0, east_id),
            col(1, west_id),
            row(0, south_slot, south_dev),
            row(1, north_slot, north_dev),
        ]

    def wait_edges(step, l):
        for slot in range(2):
            pltpu.make_async_remote_copy(
                src_ref=col_send.at[step, l],
                dst_ref=col_recv.at[step, l, slot],
                send_sem=send_sem.at[step, l, slot],
                recv_sem=recv_sem.at[step, l, slot],
                device_id={"lon": east_id},
                device_id_type=MESH,
            ).wait_recv()
            pltpu.make_async_remote_copy(
                src_ref=row_send.at[step, l, slot],
                dst_ref=row_recv.at[step, l, slot],
                send_sem=send_sem.at[step, l, 2 + slot],
                recv_sem=recv_sem.at[step, l, 2 + slot],
                device_id={"lon": east_id},
                device_id_type=MESH,
            ).wait_recv()
        for v in range(2):
            col_mix[step, l, v] = jnp.where(
                even8,
                pltpu.roll(col_recv[step, l, 1, v], cols - 1, 1),
                pltpu.roll(col_recv[step, l, 0, v], 1, 1),
            )

    def halo_lanes(packed, slot, c):
        parts = []
        for j in range(CHUNK // 8):
            t = c * (CHUNK // 8) + j
            parts.append(pltpu.roll(packed, cols - (32 * (slot // 2) + 2 * t + 1), 1))
        return jnp.concatenate(parts, axis=0)

    def numbers(l, g):
        return spread[lev * levels + l, g], 0.04 * (1.0 + category[g].astype(F32))

    def fix_rows(step, l, src, out):
        v_south = row_recv[0, l, 0, grains : grains + 1, :]
        v_south = jnp.where(is_south, jnp.zeros_like(v_south), v_south)
        to_south, from_own = jnp.maximum(v_south, 0.0), jnp.minimum(v_south, 0.0)
        to_north = coef[l, 2, rows - 1 : rows, :]
        for g in range(grains):
            m, _ = numbers(l, g)
            first, last = out(g, pl.ds(0, 1)), out(g, pl.ds(rows - 1, 1))
            x = src[grains * l + g, PAD : PAD + 1, :]
            ref, at = first
            ref[at] = (
                ref[at] + (to_south + m) * row_recv[step, l, 0, g : g + 1, :] + from_own * x
            )
            ref, at = last
            ref[at] = ref[at] + (to_north + m) * row_recv[step, l, 1, g : g + 1, :]

    def fix_cols(step, l, c, src, out):
        base = pl.multiple_of(c * CHUNK, CHUNK)
        mid = pl.ds(PAD + base, CHUNK)
        plain = pl.ds(base, CHUNK)
        u_west = halo_lanes(col_mix[0, l, 0], 6, c)
        rate = jnp.where(first_lane, jnp.maximum(u_west, 0.0), coef[l, 0, plain, :])
        from_own = jnp.where(first_lane, jnp.minimum(u_west, 0.0), 0.0)
        ends = first_lane | last_lane
        for g in range(grains):
            m, f = numbers(l, g)
            x = src[grains * l + g, mid, :]
            edge = halo_lanes(col_mix[step, l, g % 2], g, c)
            ref, at = out(g, plain)
            new = ref[at] + jnp.where(ends, (rate + m) * edge + from_own * x, 0.0)
            if l == levels - 1:
                new = new + f * src[grains * levels + g, mid, :]
            ref[at] = new

    def advance(step, l, c, src, store):
        base = pl.multiple_of(c * CHUNK, CHUNK)
        mid = pl.ds(PAD + base, CHUNK)
        plain = pl.ds(base, CHUNK)
        if step == 0:
            ue = face[l, plain, :]
            uw = jnp.where(first_lane, 0.0, pltpu.roll(ue, 1, 1))
            vn = vpad[l, mid, :]
            vs = vpad[l, pl.ds(PAD - 1 + base, CHUNK), :]
            pe, pw = -jnp.minimum(ue, 0.0), jnp.maximum(uw, 0.0)
            pn, ps = -jnp.minimum(vn, 0.0), jnp.maximum(vs, 0.0)
            own = (
                1.0
                - jnp.maximum(ue, 0.0)
                + jnp.minimum(uw, 0.0)
                - jnp.maximum(vn, 0.0)
                + jnp.minimum(vs, 0.0)
            )
            for j, value in enumerate((pe, pw, pn, ps, own)):
                coef[l, j, plain, :] = value
        else:
            pe, pw, pn, ps, own = (coef[l, j, plain, :] for j in range(5))
        offset = (l * rows + base) * cols
        hits = [cell == ids[s] - offset for s in range(vents)]
        for g in range(grains):
            i = grains * l + g
            x = src[i, mid, :]
            south = src[i, pl.ds(PAD - 1 + base, CHUNK), :]
            north = src[i, pl.ds(PAD + 1 + base, CHUNK), :]
            west = jnp.where(first_lane, 0.0, pltpu.roll(x, 1, 1))
            east = jnp.where(last_lane, 0.0, pltpu.roll(x, cols - 1, 1))
            m, f = numbers(l, g)
            new = (
                (own - (4.0 * m + f)) * x
                + (pe + m) * east
                + (pw + m) * west
                + (pn + m) * north
                + (ps + m) * south
            )
            if l < levels - 1:
                new = new + f * src[i + grains, mid, :]
            erupt = jnp.zeros_like(new)
            for s in range(vents):
                erupt = jnp.where(hits[s], vent_amount[s, g], erupt)
            store(g, mid, plain, new + erupt)

    def above_copy(step, src):
        return pltpu.make_async_remote_copy(
            src_ref=src.at[pl.ds(0, grains), pl.ds(PAD, rows)],
            dst_ref=src.at[pl.ds(levels * grains, grains), pl.ds(PAD, rows)],
            send_sem=above_send.at[step],
            recv_sem=above_recv.at[step],
            device_id={"lev": 1 - lev},
            device_id_type=MESH,
        )

    def rad_copy(c):
        part = pl.ds(pl.multiple_of(c * CHUNK, CHUNK), CHUNK)
        return pltpu.make_async_remote_copy(
            src_ref=sent_rad.at[:, part],
            dst_ref=lower_rad.at[:, part],
            send_sem=rad_send.at[c],
            recv_sem=rad_recv.at[c],
            device_id={"lev": 1 - lev},
            device_id_type=MESH,
        )

    for copy in loads:
        copy.wait()

    @pl.when(is_north)
    def _():
        for l in range(levels):
            vpad[l, PAD + rows - 1 : PAD + rows, :] = jnp.zeros((1, cols), F32)

    def loop(body):
        def turn(c, carry):
            body(c)
            return carry

        lax.fori_loop(0, chunks, turn, 0)

    def out_b(l):
        def place(g, part):
            shifted = pl.ds(part.start + PAD, part.size)
            return dens_b, (grains * l + g, shifted, slice(None))

        return place

    def out_settled(l):
        return lambda g, part: (settled, (g, l, part, slice(None)))

    def run(step, l, src, out):
        def store(g, mid, plain, value):
            ref, at = out(g, plain)
            ref[at] = value

        loop(lambda c: advance(step, l, c, src, store))

    for l in range(levels):
        pack(0, l, dens_a)
    for l in range(levels):
        run(0, l, dens_a, out_b(l))
    pl.semaphore_wait(barrier, 5)
    for l in range(levels):
        for copy in edge_copies(0, l):
            copy.start()

    @pl.when(lev == 1)
    def _():
        above_copy(0, dens_a).start()

    for l in range(levels):
        wait_edges(0, l)
        if l == levels - 1:

            @pl.when(lev == 0)
            def _():
                above_copy(0, dens_a).wait_recv()

        fix_rows(0, l, dens_a, out_b(l))
        loop(lambda c, l=l: fix_cols(0, l, c, dens_a, out_b(l)))
        pack(1, l, dens_b)
        for copy in edge_copies(1, l):
            copy.start()
        if l == 0:

            @pl.when(lev == 1)
            def _():
                above_copy(1, dens_b).start()

    def fourth(value):
        ratio = value / 250.0
        squared = ratio * ratio
        return squared * squared

    def finish(c, below):
        plain = pl.ds(pl.multiple_of(c * CHUNK, CHUNK), CHUNK)
        warm = [fourth(air[l, plain, :]) for l in range(levels)]
        for b in range(bands):
            rad = below(b, plain)
            for l in range(levels):
                rad = warm[l] + trans[b, l, plain, :] * (rad - warm[l])
                upward[b, l, plain, :] = share[b] * rad
            sent_rad[b, plain, :] = rad

    for copy in late:
        copy.wait()
    for l in range(levels):
        run(1, l, dens_b, out_settled(l))
    for l in range(levels):
        wait_edges(1, l)
        if l == levels - 1:

            @pl.when(lev == 0)
            def _():
                above_copy(1, dens_b).wait_recv()

        fix_rows(1, l, dens_b, out_settled(l))

        def second(c, l=l):
            fix_cols(1, l, c, dens_b, out_settled(l))
            plain = pl.ds(pl.multiple_of(c * CHUNK, CHUNK), CHUNK)
            field = [settled[g, l, plain, :] for g in range(grains)]
            for b in range(bands):
                optical = depth[b, 0] * field[0]
                for g in range(1, grains):
                    optical = optical + depth[b, g] * field[g]
                trans[b, l, plain, :] = jnp.exp(-optical)
            if l == levels - 1:

                @pl.when(lev == 0)
                def _():
                    heat = fourth(ground[plain, :])
                    finish(c, lambda b, part: heat)
                    rad_copy(c).start()

        loop(second)

    @pl.when(lev == 1)
    def _():
        def last(c):
            rad_copy(c).wait_recv()
            finish(c, lambda b, part: lower_rad[b, part, :])

        loop(last)

    for step in range(STEPS):
        for l in range(levels):
            for copy in edge_copies(step, l):
                copy.wait_send()

    @pl.when(lev == 1)
    def _():
        above_copy(0, dens_a).wait_send()
        above_copy(1, dens_b).wait_send()

    @pl.when(lev == 0)
    def _():
        loop(lambda c: rad_copy(c).wait_send())


def write_out(settled, upward, settled_out, upward_out, sem):
    copies = [
        pltpu.make_async_copy(settled, settled_out, sem.at[0]),
        pltpu.make_async_copy(upward, upward_out, sem.at[1]),
    ]
    for copy in copies:
        copy.start()
    for copy in copies:
        copy.wait()


def per_device(sizes, *args):
    (ash, face, spread, category, vrow, vcol, vlev, amount, depth, share, air, ground) = args
    grains, levels, rows, cols = ash.shape
    bands = depth.shape[0]
    vmem = pl.BlockSpec(memory_space=pltpu.VMEM)
    slots = (levels + 1) * grains
    scratch = [
        pltpu.VMEM((levels, rows, cols), F32),
        pltpu.VMEM((levels, rows, cols), F32),
        pltpu.VMEM((rows, cols), F32),
        pltpu.VMEM((slots, rows + 2 * PAD, cols), F32),
        pltpu.VMEM((slots, rows + 2 * PAD, cols), F32),
        pltpu.VMEM((levels, rows + 2 * PAD, cols), F32),
        pltpu.VMEM((levels, 5, rows, cols), F32),
        pltpu.VMEM((bands, levels, rows, cols), F32),
        pltpu.VMEM((bands, rows, cols), F32),
        pltpu.VMEM((bands, rows, cols), F32),
        pltpu.VMEM((STEPS, levels, 2, 8, cols), F32),
        pltpu.VMEM((STEPS, levels, 2, 2, 8, cols), F32),
        pltpu.VMEM((STEPS, levels, 2, 8, cols), F32),
        pltpu.VMEM((STEPS, levels, 2, 8, cols), F32),
        pltpu.VMEM((STEPS, levels, 2, 8, cols), F32),
        pltpu.SMEM(amount.shape, F32),
        pltpu.SemaphoreType.DMA((levels + 4,)),
        pltpu.SemaphoreType.DMA((STEPS, levels, 4)),
        pltpu.SemaphoreType.DMA((STEPS, levels, 4)),
        pltpu.SemaphoreType.DMA((STEPS,)),
        pltpu.SemaphoreType.DMA((STEPS,)),
        pltpu.SemaphoreType.DMA((rows // CHUNK,)),
        pltpu.SemaphoreType.DMA((rows // CHUNK,)),
    ]
    smalls = (spread.T, category, vrow, vcol, vlev, amount, depth, share)
    scratch += [pltpu.SMEM(small.shape, small.dtype) for small in smalls]
    scratch.append(pltpu.SemaphoreType.DMA((len(smalls),)))
    hbm = pl.BlockSpec(memory_space=pltpu.HBM)
    held = pl.pallas_call(
        functools.partial(kernel, sizes),
        out_shape=(
            pltpu.VMEM(ash.shape, F32),
            pltpu.VMEM((bands, levels, rows, cols), F32),
        ),
        in_specs=[hbm] * (4 + len(smalls)),
        out_specs=(vmem, vmem),
        scratch_shapes=scratch,
        compiler_params=pltpu.CompilerParams(
            collective_id=0, has_side_effects=True, vmem_limit_bytes=32 * 1024 * 1024
        ),
    )(*[pltpu.with_memory_space_constraint(x, pltpu.HBM) for x in (ash, face, air, ground, *smalls)])
    return pl.pallas_call(
        write_out,
        out_shape=[jax.ShapeDtypeStruct(x.shape, F32) for x in held],
        in_specs=[vmem] * 2,
        out_specs=[pl.BlockSpec(memory_space=pl.ANY)] * 2,
        scratch_shapes=[pltpu.SemaphoreType.DMA((2,))],
    )(*[pltpu.with_memory_space_constraint(x, pltpu.VMEM) for x in held])


def solution(mesh):
    sizes = (mesh.shape["lon"], mesh.shape["lat"])
    field = P("members", "lev", "lat", "lon")
    placed = (
        field,
        P(None, "lev", "lat", "lon"),
        P(),
        P(),
        P("members"),
        P("members"),
        P("members"),
        P("members", None),
        P(),
        P(),
        P("lev", "lat", "lon"),
        P("lat", "lon"),
    )
    return jax.shard_map(
        functools.partial(per_device, sizes),
        mesh=mesh,
        in_specs=placed,
        out_specs=(field, field),
        check_vma=False,
    )
```

```python
import functools

import jax
import jax.numpy as jnp
from jax import lax
from jax.experimental import pallas as pl
from jax.experimental.pallas import tpu as pltpu
from jax.sharding import PartitionSpec as P

MESH = pl.DeviceIdType.MESH
STEPS = 2
PAD = 8
CHUNK = 32
F32 = jnp.float32


def kernel(
    sizes,
    ash,
    face_hbm,
    air_hbm,
    ground_hbm,
    *rest,
):
    smalls, rest = rest[:8], rest[8:]
    small_copies, rest = rest[-9:-1], rest[:-9] + rest[-1:]
    body(sizes, ash, face_hbm, air_hbm, ground_hbm, smalls, *small_copies, *rest)


def body(
    sizes,
    ash,
    face_hbm,
    air_hbm,
    ground_hbm,
    smalls,
    spread,
    category,
    vent_row,
    vent_col,
    vent_lev,
    amount,
    depth,
    share,
    settled,
    upward,
    face,
    air,
    ground,
    dens_a,
    dens_b,
    vpad,
    coef,
    trans,
    lower_rad,
    sent_rad,
    col_send,
    col_recv,
    col_mix,
    row_send,
    row_recv,
    vent_amount,
    load_sem,
    send_sem,
    recv_sem,
    above_send,
    above_recv,
    rad_send,
    rad_recv,
    small_sem,
):
    lon_n, lat_n = sizes
    grains, levels, rows, cols = ash.shape
    bands = depth.shape[0]
    vents = amount.shape[0]
    chunks = rows // CHUNK
    tiles = rows // 8
    lon = lax.axis_index("lon")
    lat = lax.axis_index("lat")
    lev = lax.axis_index("lev")
    is_south = lat == 0
    is_north = lat == lat_n - 1
    east_id = lax.rem(lon + 1, lon_n)
    west_id = lax.rem(lon + lon_n - 1, lon_n)
    partner = lax.rem(lon + lon_n // 2, lon_n)
    north_dev = {
        "lon": jnp.where(is_north, partner, lon),
        "lat": jnp.where(is_north, lat, lat + 1),
    }
    south_dev = {
        "lon": jnp.where(is_south, partner, lon),
        "lat": jnp.where(is_south, lat, lat - 1),
    }
    north_slot = jnp.where(is_north, 1, 0)
    south_slot = jnp.where(is_south, 0, 1)

    barrier = pltpu.get_barrier_semaphore()
    for dev in ({"lon": east_id}, {"lon": west_id}, north_dev, south_dev, {"lev": 1 - lev}):
        pl.semaphore_signal(barrier, inc=1, device_id=dev, device_id_type=MESH)

    loads = []
    for l in range(levels):
        loads.append(
            pltpu.make_async_copy(
                ash.at[:, l], dens_a.at[pl.ds(grains * l, grains), pl.ds(PAD, rows)], load_sem.at[l]
            )
        )
    loads.append(
        pltpu.make_async_copy(face_hbm.at[1], vpad.at[:, pl.ds(PAD, rows)], load_sem.at[levels])
    )
    loads.append(pltpu.make_async_copy(face_hbm.at[0], face, load_sem.at[levels + 1]))
    late = [
        pltpu.make_async_copy(air_hbm, air, load_sem.at[levels + 2]),
        pltpu.make_async_copy(ground_hbm, ground, load_sem.at[levels + 3]),
    ]
    held = (spread, category, vent_row, vent_col, vent_lev, amount, depth, share)
    little = [
        pltpu.make_async_copy(source, target, small_sem.at[n])
        for n, (source, target) in enumerate(zip(smalls, held))
    ]
    for copy in loads + little + late:
        copy.start()

    for copy in little:
        copy.wait()

    ids = []
    for s in range(vents):
        r = vent_row[s] - lat * rows
        c = vent_col[s] - lon * cols
        k = vent_lev[s] - lev * levels
        inside = (r >= 0) & (r < rows) & (c >= 0) & (c < cols) & (k >= 0) & (k < levels)
        ids.append(jnp.where(inside, (k * rows + r) * cols + c, -1))
    for s in range(vents):
        for g in range(grains):
            total = amount[s, g]
            for o in range(vents):
                if o != s:
                    total = total + jnp.where(ids[o] == ids[s], amount[o, g], 0.0)
            vent_amount[s, g] = total

    lane = lax.broadcasted_iota(jnp.int32, (CHUNK, cols), 1)
    first_lane = lane == 0
    last_lane = lane == cols - 1
    lane8 = lax.broadcasted_iota(jnp.int32, (8, cols), 1)
    pair8 = lane8 // 2
    even8 = lax.rem(lane8, 2) == 0
    cell = lax.broadcasted_iota(jnp.int32, (CHUNK, cols), 0) * cols + lane

    no_row = jnp.zeros((1, cols), F32)
    for l in range(levels):
        vpad[l, PAD - 1 : PAD, :] = no_row
        for g in range(grains):
            for dens in (dens_a, dens_b):
                dens[grains * l + g, PAD - 1 : PAD, :] = no_row
                dens[grains * l + g, PAD + rows : PAD + rows + 1, :] = no_row

    @pl.when(lev == 1)
    def _():
        zero = jnp.zeros((rows, cols), F32)
        for g in range(grains):
            dens_a[levels * grains + g, pl.ds(PAD, rows), :] = zero
            dens_b[levels * grains + g, pl.ds(PAD, rows), :] = zero

    def pack(step, l, src):
        def turn(t, carry):
            p0, p1 = carry
            at = pl.ds(pl.multiple_of(PAD + 8 * t, 8), 8)
            for q in range(3):
                here = pair8 == 16 * q + t
                move = 32 * q + 2 * t + 1
                p0 = jnp.where(here, pltpu.roll(src[grains * l + 2 * q, at, :], move, 1), p0)
                p1 = jnp.where(here, pltpu.roll(src[grains * l + 2 * q + 1, at, :], move, 1), p1)
            if step == 0:
                here = pair8 == 48 + t
                u = face[l, pl.ds(pl.multiple_of(8 * t, 8), 8), :]
                p0 = jnp.where(here, pltpu.roll(u, 97 + 2 * t, 1), p0)
            return p0, p1

        zero = jnp.zeros((8, cols), F32)
        p0, p1 = lax.fori_loop(0, tiles, turn, (zero, zero), unroll=4)
        col_send[step, l, 0] = p0
        col_send[step, l, 1] = p1
        for g in range(grains):
            row_send[step, l, 0, g : g + 1, :] = src[grains * l + g, PAD : PAD + 1, :]
            row_send[step, l, 1, g : g + 1, :] = src[
                grains * l + g, PAD + rows - 1 : PAD + rows, :
            ]
        if step == 0:
            row_send[step, l, 1, grains : grains + 1, :] = vpad[
                l, PAD + rows - 1 : PAD + rows, :
            ]

    def edge_copies(step, l):
        def col(slot, dev):
            return pltpu.make_async_remote_copy(
                src_ref=col_send.at[step, l],
                dst_ref=col_recv.at[step, l, slot],
                send_sem=send_sem.at[step, l, slot],
                recv_sem=recv_sem.at[step, l, slot],
                device_id={"lon": dev},
                device_id_type=MESH,
            )

        def row(edge, slot, dev):
            return pltpu.make_async_remote_copy(
                src_ref=row_send.at[step, l, edge],
                dst_ref=row_recv.at[step, l, slot],
                send_sem=send_sem.at[step, l, 2 + edge],
                recv_sem=recv_sem.at[step, l, 2 + slot],
                device_id=dev,
                device_id_type=MESH,
            )

        return [
            col(0, east_id),
            col(1, west_id),
            row(0, south_slot, south_dev),
            row(1, north_slot, north_dev),
        ]

    def wait_edges(step, l):
        for slot in range(2):
            pltpu.make_async_remote_copy(
                src_ref=col_send.at[step, l],
                dst_ref=col_recv.at[step, l, slot],
                send_sem=send_sem.at[step, l, slot],
                recv_sem=recv_sem.at[step, l, slot],
                device_id={"lon": east_id},
                device_id_type=MESH,
            ).wait_recv()
            pltpu.make_async_remote_copy(
                src_ref=row_send.at[step, l, slot],
                dst_ref=row_recv.at[step, l, slot],
                send_sem=send_sem.at[step, l, 2 + slot],
                recv_sem=recv_sem.at[step, l, 2 + slot],
                device_id={"lon": east_id},
                device_id_type=MESH,
            ).wait_recv()
        for v in range(2):
            col_mix[step, l, v] = jnp.where(
                even8,
                pltpu.roll(col_recv[step, l, 1, v], cols - 1, 1),
                pltpu.roll(col_recv[step, l, 0, v], 1, 1),
            )

    def halo_lanes(packed, slot, c):
        parts = []
        for j in range(CHUNK // 8):
            t = c * (CHUNK // 8) + j
            parts.append(pltpu.roll(packed, cols - (32 * (slot // 2) + 2 * t + 1), 1))
        return jnp.concatenate(parts, axis=0)

    def numbers(l, g):
        return spread[lev * levels + l, g], 0.04 * (1.0 + category[g].astype(F32))

    def fix_rows(step, l, src, out):
        v_south = row_recv[0, l, 0, grains : grains + 1, :]
        v_south = jnp.where(is_south, jnp.zeros_like(v_south), v_south)
        to_south, from_own = jnp.maximum(v_south, 0.0), jnp.minimum(v_south, 0.0)
        to_north = coef[l, 2, rows - 1 : rows, :]
        for g in range(grains):
            m, _ = numbers(l, g)
            first, last = out(g, pl.ds(0, 1)), out(g, pl.ds(rows - 1, 1))
            x = src[grains * l + g, PAD : PAD + 1, :]
            ref, at = first
            ref[at] = (
                ref[at] + (to_south + m) * row_recv[step, l, 0, g : g + 1, :] + from_own * x
            )
            ref, at = last
            ref[at] = ref[at] + (to_north + m) * row_recv[step, l, 1, g : g + 1, :]

    def fix_cols(step, l, c, src, out):
        base = pl.multiple_of(c * CHUNK, CHUNK)
        mid = pl.ds(PAD + base, CHUNK)
        plain = pl.ds(base, CHUNK)
        u_west = halo_lanes(col_mix[0, l, 0], 6, c)
        rate = jnp.where(first_lane, jnp.maximum(u_west, 0.0), coef[l, 0, plain, :])
        from_own = jnp.where(first_lane, jnp.minimum(u_west, 0.0), 0.0)
        ends = first_lane | last_lane
        for g in range(grains):
            m, f = numbers(l, g)
            x = src[grains * l + g, mid, :]
            edge = halo_lanes(col_mix[step, l, g % 2], g, c)
            ref, at = out(g, plain)
            new = ref[at] + jnp.where(ends, (rate + m) * edge + from_own * x, 0.0)
            if l == levels - 1:
                new = new + f * src[grains * levels + g, mid, :]
            ref[at] = new

    def advance(step, l, c, src, store):
        base = pl.multiple_of(c * CHUNK, CHUNK)
        mid = pl.ds(PAD + base, CHUNK)
        plain = pl.ds(base, CHUNK)
        if step == 0:
            ue = face[l, plain, :]
            uw = jnp.where(first_lane, 0.0, pltpu.roll(ue, 1, 1))
            vn = vpad[l, mid, :]
            vs = vpad[l, pl.ds(PAD - 1 + base, CHUNK), :]
            pe, pw = -jnp.minimum(ue, 0.0), jnp.maximum(uw, 0.0)
            pn, ps = -jnp.minimum(vn, 0.0), jnp.maximum(vs, 0.0)
            own = (
                1.0
                - jnp.maximum(ue, 0.0)
                + jnp.minimum(uw, 0.0)
                - jnp.maximum(vn, 0.0)
                + jnp.minimum(vs, 0.0)
            )
            for j, value in enumerate((pe, pw, pn, ps, own)):
                coef[l, j, plain, :] = value
        else:
            pe, pw, pn, ps, own = (coef[l, j, plain, :] for j in range(5))
        offset = (l * rows + base) * cols
        hits = [cell == ids[s] - offset for s in range(vents)]
        for g in range(grains):
            i = grains * l + g
            x = src[i, mid, :]
            south = src[i, pl.ds(PAD - 1 + base, CHUNK), :]
            north = src[i, pl.ds(PAD + 1 + base, CHUNK), :]
            west = jnp.where(first_lane, 0.0, pltpu.roll(x, 1, 1))
            east = jnp.where(last_lane, 0.0, pltpu.roll(x, cols - 1, 1))
            m, f = numbers(l, g)
            new = (
                (own - (4.0 * m + f)) * x
                + (pe + m) * east
                + (pw + m) * west
                + (pn + m) * north
                + (ps + m) * south
            )
            if l < levels - 1:
                new = new + f * src[i + grains, mid, :]
            erupt = jnp.zeros_like(new)
            for s in range(vents):
                erupt = jnp.where(hits[s], vent_amount[s, g], erupt)
            store(g, mid, plain, new + erupt)

    def above_copy(step, src):
        return pltpu.make_async_remote_copy(
            src_ref=src.at[pl.ds(0, grains), pl.ds(PAD, rows)],
            dst_ref=src.at[pl.ds(levels * grains, grains), pl.ds(PAD, rows)],
            send_sem=above_send.at[step],
            recv_sem=above_recv.at[step],
            device_id={"lev": 1 - lev},
            device_id_type=MESH,
        )

    def rad_copy(c):
        part = pl.ds(pl.multiple_of(c * CHUNK, CHUNK), CHUNK)
        return pltpu.make_async_remote_copy(
            src_ref=sent_rad.at[:, part],
            dst_ref=lower_rad.at[:, part],
            send_sem=rad_send.at[c],
            recv_sem=rad_recv.at[c],
            device_id={"lev": 1 - lev},
            device_id_type=MESH,
        )

    for copy in loads:
        copy.wait()

    @pl.when(is_north)
    def _():
        for l in range(levels):
            vpad[l, PAD + rows - 1 : PAD + rows, :] = jnp.zeros((1, cols), F32)

    def loop(body):
        def turn(c, carry):
            body(c)
            return carry

        lax.fori_loop(0, chunks, turn, 0)

    def out_b(l):
        def place(g, part):
            shifted = pl.ds(part.start + PAD, part.size)
            return dens_b, (grains * l + g, shifted, slice(None))

        return place

    def out_settled(l):
        return lambda g, part: (settled, (g, l, part, slice(None)))

    def run(step, l, src, out):
        def store(g, mid, plain, value):
            ref, at = out(g, plain)
            ref[at] = value

        loop(lambda c: advance(step, l, c, src, store))

    for l in range(levels):
        pack(0, l, dens_a)
    pl.semaphore_wait(barrier, 5)
    for l in range(levels):
        for copy in edge_copies(0, l):
            copy.start()

    @pl.when(lev == 1)
    def _():
        above_copy(0, dens_a).start()

    for l in range(levels):
        run(0, l, dens_a, out_b(l))
    for l in range(levels):
        wait_edges(0, l)
        if l == levels - 1:

            @pl.when(lev == 0)
            def _():
                above_copy(0, dens_a).wait_recv()

        fix_rows(0, l, dens_a, out_b(l))
        loop(lambda c, l=l: fix_cols(0, l, c, dens_a, out_b(l)))
        pack(1, l, dens_b)
        for copy in edge_copies(1, l):
            copy.start()
        if l == 0:

            @pl.when(lev == 1)
            def _():
                above_copy(1, dens_b).start()

    def fourth(value):
        ratio = value / 250.0
        squared = ratio * ratio
        return squared * squared

    def finish(c, below):
        plain = pl.ds(pl.multiple_of(c * CHUNK, CHUNK), CHUNK)
        warm = [fourth(air[l, plain, :]) for l in range(levels)]
        for b in range(bands):
            rad = below(b, plain)
            for l in range(levels):
                rad = warm[l] + trans[b, l, plain, :] * (rad - warm[l])
                upward[b, l, plain, :] = share[b] * rad
            sent_rad[b, plain, :] = rad

    for copy in late:
        copy.wait()
    for l in range(levels):
        run(1, l, dens_b, out_settled(l))
    for l in range(levels):
        wait_edges(1, l)
        if l == levels - 1:

            @pl.when(lev == 0)
            def _():
                above_copy(1, dens_b).wait_recv()

        fix_rows(1, l, dens_b, out_settled(l))

        def second(c, l=l):
            fix_cols(1, l, c, dens_b, out_settled(l))
            plain = pl.ds(pl.multiple_of(c * CHUNK, CHUNK), CHUNK)
            field = [settled[g, l, plain, :] for g in range(grains)]
            for b in range(bands):
                optical = depth[b, 0] * field[0]
                for g in range(1, grains):
                    optical = optical + depth[b, g] * field[g]
                trans[b, l, plain, :] = jnp.exp(-optical)
            if l == levels - 1:

                @pl.when(lev == 0)
                def _():
                    heat = fourth(ground[plain, :])
                    finish(c, lambda b, part: heat)
                    rad_copy(c).start()

        loop(second)

    @pl.when(lev == 1)
    def _():
        def last(c):
            rad_copy(c).wait_recv()
            finish(c, lambda b, part: lower_rad[b, part, :])

        loop(last)

    for step in range(STEPS):
        for l in range(levels):
            for copy in edge_copies(step, l):
                copy.wait_send()

    @pl.when(lev == 1)
    def _():
        above_copy(0, dens_a).wait_send()
        above_copy(1, dens_b).wait_send()

    @pl.when(lev == 0)
    def _():
        loop(lambda c: rad_copy(c).wait_send())


def write_out(settled, upward, settled_out, upward_out, sem):
    copies = [
        pltpu.make_async_copy(settled, settled_out, sem.at[0]),
        pltpu.make_async_copy(upward, upward_out, sem.at[1]),
    ]
    for copy in copies:
        copy.start()
    for copy in copies:
        copy.wait()


def per_device(sizes, *args):
    (ash, face, spread, category, vrow, vcol, vlev, amount, depth, share, air, ground) = args
    grains, levels, rows, cols = ash.shape
    bands = depth.shape[0]
    vmem = pl.BlockSpec(memory_space=pltpu.VMEM)
    slots = (levels + 1) * grains
    scratch = [
        pltpu.VMEM((levels, rows, cols), F32),
        pltpu.VMEM((levels, rows, cols), F32),
        pltpu.VMEM((rows, cols), F32),
        pltpu.VMEM((slots, rows + 2 * PAD, cols), F32),
        pltpu.VMEM((slots, rows + 2 * PAD, cols), F32),
        pltpu.VMEM((levels, rows + 2 * PAD, cols), F32),
        pltpu.VMEM((levels, 5, rows, cols), F32),
        pltpu.VMEM((bands, levels, rows, cols), F32),
        pltpu.VMEM((bands, rows, cols), F32),
        pltpu.VMEM((bands, rows, cols), F32),
        pltpu.VMEM((STEPS, levels, 2, 8, cols), F32),
        pltpu.VMEM((STEPS, levels, 2, 2, 8, cols), F32),
        pltpu.VMEM((STEPS, levels, 2, 8, cols), F32),
        pltpu.VMEM((STEPS, levels, 2, 8, cols), F32),
        pltpu.VMEM((STEPS, levels, 2, 8, cols), F32),
        pltpu.SMEM(amount.shape, F32),
        pltpu.SemaphoreType.DMA((levels + 4,)),
        pltpu.SemaphoreType.DMA((STEPS, levels, 4)),
        pltpu.SemaphoreType.DMA((STEPS, levels, 4)),
        pltpu.SemaphoreType.DMA((STEPS,)),
        pltpu.SemaphoreType.DMA((STEPS,)),
        pltpu.SemaphoreType.DMA((rows // CHUNK,)),
        pltpu.SemaphoreType.DMA((rows // CHUNK,)),
    ]
    smalls = (spread.T, category, vrow, vcol, vlev, amount, depth, share)
    scratch += [pltpu.SMEM(small.shape, small.dtype) for small in smalls]
    scratch.append(pltpu.SemaphoreType.DMA((len(smalls),)))
    hbm = pl.BlockSpec(memory_space=pltpu.HBM)
    held = pl.pallas_call(
        functools.partial(kernel, sizes),
        out_shape=(
            pltpu.VMEM(ash.shape, F32),
            pltpu.VMEM((bands, levels, rows, cols), F32),
        ),
        in_specs=[hbm] * (4 + len(smalls)),
        out_specs=(vmem, vmem),
        scratch_shapes=scratch,
        compiler_params=pltpu.CompilerParams(
            collective_id=0, has_side_effects=True, vmem_limit_bytes=32 * 1024 * 1024
        ),
    )(*[pltpu.with_memory_space_constraint(x, pltpu.HBM) for x in (ash, face, air, ground, *smalls)])
    return pl.pallas_call(
        write_out,
        out_shape=[jax.ShapeDtypeStruct(x.shape, F32) for x in held],
        in_specs=[vmem] * 2,
        out_specs=[pl.BlockSpec(memory_space=pl.ANY)] * 2,
        scratch_shapes=[pltpu.SemaphoreType.DMA((2,))],
    )(*[pltpu.with_memory_space_constraint(x, pltpu.VMEM) for x in held])


def solution(mesh):
    sizes = (mesh.shape["lon"], mesh.shape["lat"])
    field = P("members", "lev", "lat", "lon")
    placed = (
        field,
        P(None, "lev", "lat", "lon"),
        P(),
        P(),
        P("members"),
        P("members"),
        P("members"),
        P("members", None),
        P(),
        P(),
        P("lev", "lat", "lon"),
        P("lat", "lon"),
    )
    return jax.shard_map(
        functools.partial(per_device, sizes),
        mesh=mesh,
        in_specs=placed,
        out_specs=(field, field),
        check_vma=False,
    )
```
